1024 devices in a mesh: dp: 128 (over y, z, core), expert: 8 (over x).
Axes of the slice: x: 8, y: 8, z: 8, core: 2. Of those that a mesh axis runs over, the one named last changes fastest.
Arguments:
- grad_partial: bfloat16 [8, 12, 256, 16384], P('expert', None, None, 'dp'), may hold values from -2.5 to 2.5
- momentum: float32 [16, 256, 16384], P('expert', None, 'dp'), may hold values from -12 to 12
- owner: int32 [12], replicated, may hold values from 0 to 7, as said below
Outputs:
- new_momentum: float32 [16, 256, 16384], P('expert', None, 'dp')
- update: float32 [12, 256, 16384], P(None, 'expert', 'dp')
The draws below stay inside these ranges and needn't reach their ends.
Inputs may be any that keep to these rules, and one draw needn't show every extreme that they name: No owner index is named by more than 2 layers, and at least one is named by exactly 2.
All inputs are finite; a program needn't handle non-finite values.
Results may differ from the reference program's by a relative error of at most 0.0003.
Values sent between devices are 32-bit elements; how exact they have to be, the bound alone decides.
A program may use at most 128 MiB of HBM per device.

```python
import math
import jax
import jax.numpy as jnp
from jax import lax

R = 256
N = 16384
CAP = 2
ITERS = 3
SLOTS = 16
LAYERS = 12
N_EXPERT = 8


def draw_owner(key, part):
    key = jax.random.fold_in(key, 11)
    key = jax.random.fold_in(key, part)
    first_key, second_key, third_key = jax.random.split(key, 3)
    owners = SLOTS // CAP
    fullest = jax.random.randint(first_key, (), 0, owners).astype(jnp.int32)
    order = jax.random.permutation(second_key, LAYERS).astype(jnp.int32)
    others = (jax.random.permutation(third_key, SLOTS - CAP)[:LAYERS - CAP] // CAP).astype(jnp.int32)
    others = others + (others >= fullest).astype(jnp.int32)
    listing = jnp.concatenate([jnp.full((CAP,), 1, jnp.int32) * fullest, others])
    return listing[order]


def draw_momentum(key, part):
    key = jax.random.fold_in(key, 23)
    base_key, row_key, column_key = jax.random.split(key, 3)
    shape = (SLOTS, R, N)
    base = jnp.clip(jax.random.normal(base_key, shape, jnp.float32), -4.0, 4.0)
    row_reach = math.log(3.0)
    rows = jnp.exp(jax.random.uniform(row_key, (SLOTS, R, 1), jnp.float32, 0.0, row_reach))
    rising = jnp.power(10.0, 0.5 * jnp.arange(N, dtype=jnp.float32) / N)
    columns = rising[None, None, :] * jnp.exp(jax.random.uniform(column_key, (SLOTS, 1, N), jnp.float32, 0.0, math.log(3.16)))
    return (0.1 * base * rows * columns).astype(jnp.float32)


def strengthened(drawn, rng, source, target, shards_of, factor):
    owner, partner = [(jnp.arange(drawn.shape[dim]) // (drawn.shape[dim] // shards_of)).reshape([-1 if axis == dim else 1 for axis in range(drawn.ndim)]) for dim in (source, target)]
    chosen = jax.random.permutation(rng, shards_of)[partner]
    strong = (owner == chosen) | (owner == (partner + shards_of // 2) % shards_of)
    return jnp.where(strong, factor * drawn, drawn)


def block_levels(key, extent, cuts, smallest, top_value):
    gain, own = 1.0, jax.random.fold_in(key, 6)
    for dim, parts in cuts:
        draws = jnp.exp(jax.random.uniform(jax.random.fold_in(own, dim), (parts,), jnp.float32, smallest / len(cuts), top_value / len(cuts)))
        gain = gain * jnp.repeat(draws, extent[dim] // parts).reshape([-1 if axis == dim else 1 for axis in range(len(extent))])
    return gain


def noise_with(key, shape, deviation, reach, shards, heavy, kind=jnp.bfloat16):
    values = deviation * jax.random.normal(key, shape, jnp.float32)
    if shards:
        values = values * block_levels(key, shape, shards, -0.22, 0.18)
    return jnp.clip(strengthened(values, jax.random.fold_in(key, 3), *heavy), -reach, reach).astype(kind)


def setup_inputs(seed: int = 0) -> dict:
    arg_keys = jax.random.split(jax.random.key(seed), 4)
    return {
        "grad_partial": noise_with(arg_keys[0], (N_EXPERT, LAYERS, R, N), 0.35, 2.5, ((0, 8), (3, 128)), (0, 2, 8, 2.0)),
        "momentum": draw_momentum(jax.random.fold_in(arg_keys[3], 71), 0),
        "owner": draw_owner(jax.random.fold_in(arg_keys[3], 71), 0),
    }


momentum_rate = 0.95
epsilon = 1e-07
quintic_one = 3.4445
quintic_two = -4.775
quintic_three = 2.0315
update_gain = 0.2

def slot_positions(owner):
    count = owner.shape[0]
    same_owner = owner[:, None] == owner[None, :]
    position = jnp.arange(count, dtype=jnp.int32)
    earlier = position[:, None] > position[None, :]
    rank = lax.optimization_barrier(jnp.sum((same_owner & earlier).astype(jnp.int32), axis=1))
    return (owner * CAP + rank).astype(jnp.int32)

def reference(grad_partial, momentum, owner):

    def add_replica(index, total):
        return total + grad_partial[index].astype(jnp.float32)
    grad = lax.fori_loop(0, grad_partial.shape[0], add_replica, jnp.zeros(grad_partial.shape[1:], jnp.float32))
    slot_index = slot_positions(owner)
    owned = jnp.zeros(momentum.shape, jnp.float32).at[slot_index].set(grad)
    new_momentum = momentum_rate * momentum + owned
    field = owned + momentum_rate * new_momentum
    norms = jnp.sqrt(lax.optimization_barrier(jnp.sum(field * field, axis=(1, 2))))
    field = field / (norms + epsilon)[:, None, None]
    for step in range(ITERS):
        gram = jnp.einsum('qrn,qtn->qrt', field, field, precision=lax.Precision.HIGHEST)
        square = jnp.einsum('qrt,qtu->qru', gram, gram, precision=lax.Precision.HIGHEST)
        mixer = quintic_two * gram + quintic_three * square
        field = quintic_one * field + jnp.einsum('qrt,qtn->qrn', mixer, field, precision=lax.Precision.HIGHEST)
    update = update_gain * math.sqrt(N) * field[slot_index]
    return (new_momentum, update)
```

```python
import functools
import math

import jax
import jax.numpy as jnp
from jax import lax
from jax.experimental import pallas as pl
from jax.experimental.pallas import tpu as pltpu
from jax.sharding import PartitionSpec as P

N = 16384
CAP = 2
OWNERS = 8
LAYERS = 12
ROWS = 256
COLS = 128
HALF = ROWS // 2
BLOCK = ROWS // OWNERS
PIECE = 3 * HALF // 16

momentum_rate = 0.95
epsilon = 1e-07
quintic_one = 3.4445
quintic_two = -4.775
quintic_three = 2.0315
update_gain = 0.2

MESH = pl.DeviceIdType.MESH
FAR_FIRST = (4, 3, 5, 2, 6, 1, 7)
STEPS = 4


def split(value):
    high = value.astype(jnp.bfloat16)
    low = (value - high.astype(jnp.float32)).astype(jnp.bfloat16)
    return high, low


def dot(left, right, dims):
    return lax.dot_general(left, right, (dims, ((), ())), preferred_element_type=jnp.float32)


def product(left, right, dims=((1,), (0,))):
    cross = dot(left[0], right[1], dims) + dot(left[1], right[0], dims)
    return dot(left[0], right[0], dims) + cross


def mod8(value):
    return lax.rem(value + 16, 8)


def kernel(
    owner_ref,
    grad_hbm,
    momentum_hbm,
    new_momentum_ref,
    update_ref,
    grad_ref,
    momentum_ref,
    first_ref,
    chain_ref,
    field_ref,
    pair_ref,
    gram_ref,
    early_ref,
    early_sum_ref,
    late_ref,
    late_sum_ref,
    whole_ref,
    result_ref,
    rows_ref,
    load_sem,
    chain_send,
    chain_recv,
    pair_send,
    pair_recv,
    gram_send,
    gram_recv,
    rows_send,
    rows_recv,
    go_left,
    go_right,
    go_core,
    go_y,
    go_z,
    go_x,
):
    place = lax.axis_index("dp")
    x = lax.axis_index("expert")
    y, z, core = place // 16, lax.rem(place // 2, 8), lax.rem(place, 2)

    def device(y_, z_, core_, x_):
        return ((y_ * 8 + z_) * 2 + core_, x_)

    def signal(sem, target):
        pl.semaphore_signal(sem, inc=1, device_id=target, device_id_type=MESH)

    def each(low, high, body):
        def step(index, carry):
            body(index)
            return carry

        lax.fori_loop(low, high, step, 0)

    def await_all(sem, count):
        @pl.when(count > 0)
        def _():
            pl.semaphore_wait(sem, count)

    barrier = pltpu.get_barrier_semaphore()

    def greet_x(j):
        signal(barrier, device(y, z, 0, j))
        signal(barrier, device(y, z, 1, j))

    each(0, x, greet_x)
    each(0, y, lambda j: signal(barrier, device(j, z, core, x)))
    each(0, z, lambda j: signal(barrier, device(y, j, core, x)))
    each(0, core, lambda j: signal(barrier, device(y, z, j, x)))

    load_grad = pltpu.make_async_copy(grad_hbm.at[0], grad_ref, load_sem.at[0])
    load_momentum = pltpu.make_async_copy(momentum_hbm, momentum_ref, load_sem.at[1])
    load_grad.start()
    load_momentum.start()

    owners = [owner_ref[layer] for layer in range(LAYERS)]
    layers = []
    for ahead in range(OWNERS):
        wanted = mod8(x + ahead)
        first = jnp.int32(-1)
        second = jnp.int32(-1)
        for layer in range(LAYERS):
            hit = owners[layer] == wanted
            second = jnp.where(hit & (first >= 0), layer, second)
            first = jnp.where(hit & (first < 0), layer, first)
        layers.append((first, second))

    def share(ahead, slot, half):
        layer = layers[ahead % 8][slot]
        value = grad_ref[jnp.maximum(layer, 0), pl.ds(half * HALF, HALF), :].astype(jnp.float32)
        return jnp.where(layer >= 0, value, 0.0)

    load_grad.wait()
    await_all(barrier, 2 * (7 - x) + (7 - y) + (7 - z) + (1 - core))

    @pl.when(x < 7)
    def _():
        signal(go_left, device(y, z, core, x + 1))

    @pl.when(x == 0)
    def _():
        signal(go_right, device(y, z, core, 7))

    def go_ahead():
        each(core + 1, 2, lambda j: signal(go_core, device(y, z, j, x)))
        each(y + 1, 8, lambda j: signal(go_y, device(j, z, core, x)))
        each(z + 1, 8, lambda j: signal(go_z, device(y, j, core, x)))

        def go_to_x(j):
            signal(go_x, device(y, z, 0, j))
            signal(go_x, device(y, z, 1, j))

        each(x + 1, 8, go_to_x)

    def chain_index(direction, slot, half):
        return (direction * 2 + slot) * 2 + half

    def chain_copy(direction, slot, half, step):
        index = chain_index(direction, slot, half)
        source = first_ref.at[index] if step == 0 else chain_ref.at[index * STEPS + step - 1]
        target = mod8(x + 1) if direction == 0 else mod8(x + 7)
        return pltpu.make_async_remote_copy(
            src_ref=source,
            dst_ref=chain_ref.at[index * STEPS + step],
            send_sem=chain_send.at[index * STEPS + step],
            recv_sem=chain_recv.at[index * STEPS + step],
            device_id=device(y, z, core, target),
            device_id_type=MESH,
        )

    started = []
    for step in range(STEPS):
        for length in (4, 3):
            if step >= length:
                continue
            for slot in range(CAP):
                for direction in (0, 1):
                    half = 0 if (direction == 0) == (length == 4) else 1
                    ahead = length - step if direction == 0 else step - length
                    index = chain_index(direction, slot, half)
                    if step == 0:
                        first_ref[index] = share(ahead, slot, half)
                        if length == 4 and slot == 0:
                            if direction == 0:
                                each(0, (x == 7).astype(jnp.int32), lambda j: pl.semaphore_wait(go_right, 1))
                            else:
                                each(0, (x > 0).astype(jnp.int32), lambda j: pl.semaphore_wait(go_left, 1))
                    else:
                        chain_copy(direction, slot, half, step - 1).wait_recv()
                        at = index * STEPS + step - 1
                        chain_ref[at] = chain_ref[at] + share(ahead, slot, half)
                    copy = chain_copy(direction, slot, half, step)
                    copy.start()
                    started.append(copy)
        if step == 0:
            go_ahead()
            load_momentum.wait()

    for half in range(2):
        rows = pl.ds(half * HALF, HALF)
        for slot in range(CAP):
            lengths = (4, 3) if half == 0 else (3, 4)
            total = share(0, slot, half)
            for direction in (0, 1):
                last = lengths[direction] - 1
                chain_copy(direction, slot, half, last).wait_recv()
                total = total + chain_ref[chain_index(direction, slot, half) * STEPS + last]
            fresh = momentum_rate * momentum_ref[slot, rows, :] + total
            new_momentum_ref[slot, rows, :] = fresh
            field_ref[slot, rows, :] = total + momentum_rate * fresh

    each(0, core, lambda j: pl.semaphore_wait(go_core, 1))
    pair = pltpu.make_async_remote_copy(
        src_ref=field_ref.at[1 - core],
        dst_ref=pair_ref,
        send_sem=pair_send,
        recv_sem=pair_recv,
        device_id=device(y, z, 1 - core, x),
        device_id_type=MESH,
    )
    pair.start()
    started.append(pair)
    mine = field_ref[core]
    mine_split = split(mine)
    rows_rows = ((1,), (1,))
    gram = product(mine_split, mine_split, rows_rows)
    pair.wait_recv()
    other = pair_ref[...]
    other_split = split(other)
    gram = gram + product(other_split, other_split, rows_rows)

    stacked = jnp.concatenate([gram[:HALF, :HALF], gram[:HALF, HALF:], gram[HALF:, HALF:]], axis=0)
    gram_ref[...] = stacked.reshape(16, PIECE, HALF)
    await_all(go_y, y)
    await_all(go_z, z)

    def along(axis, ahead):
        return device(mod8(y + ahead), z, core, x) if axis == 0 else device(y, mod8(z + ahead), core, x)

    where = (y, z)

    def gram_copy(stage, order, ahead):
        axis = 1 - order if stage == 1 else order
        if stage == 0:
            source, target = gram_ref.at[order * 8 + mod8(where[order] + ahead)], early_ref.at[order, ahead - 1]
        elif stage == 1:
            source, target = early_sum_ref.at[order], late_ref.at[order, ahead - 1]
        else:
            source, target = late_sum_ref.at[order], whole_ref.at[order * 8 + where[order]]
        index = (stage * 2 + order) * 7 + ahead - 1
        return pltpu.make_async_remote_copy(
            src_ref=source,
            dst_ref=target,
            send_sem=gram_send.at[index],
            recv_sem=gram_recv.at[index],
            device_id=along(axis, ahead),
            device_id_type=MESH,
        )

    def gram_arrival(stage, order, ahead):
        if stage < 2:
            gram_copy(stage, order, ahead).wait_recv()
            return
        index = (stage * 2 + order) * 7 + ahead - 1
        pltpu.make_async_remote_copy(
            src_ref=late_sum_ref.at[order],
            dst_ref=whole_ref.at[order * 8 + mod8(where[order] - ahead)],
            send_sem=gram_send.at[index],
            recv_sem=gram_recv.at[index],
            device_id=along(order, ahead),
            device_id_type=MESH,
        ).wait_recv()

    for stage in range(3):
        if stage == 1:
            for order in range(2):
                total = gram_ref[order * 8 + where[order]]
                for ahead in range(1, 8):
                    gram_arrival(0, order, ahead)
                    total = total + early_ref[order, ahead - 1]
                early_sum_ref[order] = total
        if stage == 2:
            for order in range(2):
                total = early_sum_ref[order]
                for ahead in range(1, 8):
                    gram_arrival(1, order, ahead)
                    total = total + late_ref[order, ahead - 1]
                late_sum_ref[order] = total
                whole_ref[order * 8 + where[order]] = total
        for ahead in FAR_FIRST:
            for order in range(2):
                copy = gram_copy(stage, order, ahead)
                copy.start()
                started.append(copy)
    for order in range(2):
        for ahead in range(1, 8):
            gram_arrival(2, order, ahead)

    blocks = whole_ref[...].reshape(3 * HALF, HALF)
    corner, side, rest = blocks[:HALF], blocks[HALF : 2 * HALF], blocks[2 * HALF :]
    row = lax.broadcasted_iota(jnp.int32, (HALF, HALF), 0)
    column = lax.broadcasted_iota(jnp.int32, (HALF, HALF), 1)
    diagonal = jnp.where(row == column, corner + rest, 0.0)
    squares = jnp.sum(diagonal)
    scale = 1.0 / (jnp.sqrt(jnp.full((1, 1), squares, jnp.float32)) + epsilon)
    gram = jnp.concatenate(
        [jnp.concatenate([corner, side], axis=1), jnp.concatenate([side.T, rest], axis=1)], axis=0
    )
    gram = gram * (scale * scale)
    field = jnp.concatenate([mine * scale, other * scale], axis=1)

    for step in range(2):
        gram_split = split(gram)
        square = product(gram_split, gram_split)
        square_split = split(square)
        cube = product(gram_split, square_split)
        mixer = quintic_two * gram + quintic_three * square
        mixed = quintic_one * gram + quintic_two * square + quintic_three * cube
        mixer_split = split(mixer)
        field = quintic_one * field + product(mixer_split, split(field))
        gram = quintic_one * mixed + product(split(mixed), mixer_split)
    gram_split = split(gram)
    bent = product(gram_split, split(field))
    twice = product(gram_split, split(bent))
    gain = update_gain * math.sqrt(N)
    result = (gain * quintic_one) * field + (gain * quintic_two) * bent + (gain * quintic_three) * twice

    result_ref[0] = result[:, :COLS]
    result_ref[1] = result[:, COLS:]
    await_all(go_x, 2 * x)

    def rows_copy(ahead, other_core):
        target = mod8(x + ahead)
        index = other_core * 8 + ahead
        return pltpu.make_async_remote_copy(
            src_ref=result_ref.at[other_core, pl.ds(pl.multiple_of(target * BLOCK, BLOCK), BLOCK), :],
            dst_ref=rows_ref.at[x * 2 + core],
            send_sem=rows_send.at[index],
            recv_sem=rows_recv.at[index],
            device_id=device(y, z, core if other_core == 0 else 1 - core, target),
            device_id_type=MESH,
        )

    def rows_arrival(ahead, other_core):
        source = mod8(x - ahead)
        from_core = core if other_core == 0 else 1 - core
        index = other_core * 8 + ahead
        pltpu.make_async_remote_copy(
            src_ref=result_ref.at[other_core, pl.ds(0, BLOCK), :],
            dst_ref=rows_ref.at[source * 2 + from_core],
            send_sem=rows_send.at[index],
            recv_sem=rows_recv.at[index],
            device_id=device(y, z, from_core, mod8(x + ahead)),
            device_id_type=MESH,
        ).wait_recv()

    partners = [(ahead, other_core) for ahead in FAR_FIRST for other_core in range(2)] + [(0, 1)]
    for ahead, other_core in partners:
        copy = rows_copy(ahead, other_core)
        copy.start()
        started.append(copy)
    rows_ref[x * 2 + core] = result_ref[0, pl.ds(pl.multiple_of(x * BLOCK, BLOCK), BLOCK), :]
    slots = []
    for layer in range(LAYERS):
        rank = jnp.int32(0)
        for before in range(layer):
            rank = rank + (owners[before] == owners[layer]).astype(jnp.int32)
        slots.append(owners[layer] * CAP + rank)
    for ahead, other_core in partners:
        rows_arrival(ahead, other_core)
    for layer in range(LAYERS):
        update_ref[layer] = rows_ref[slots[layer]]
    for copy in started:
        copy.wait_send()


def on_device(grad_partial, momentum, owner):
    f32 = jnp.float32
    chains = 8 * STEPS
    dma = pltpu.SemaphoreType.DMA
    regular = pltpu.SemaphoreType.REGULAR
    return pl.pallas_call(
        kernel,
        out_shape=(
            jax.ShapeDtypeStruct((CAP, ROWS, COLS), f32),
            jax.ShapeDtypeStruct((LAYERS, BLOCK, COLS), f32),
        ),
        in_specs=[
            pl.BlockSpec(memory_space=pltpu.SMEM),
            pl.BlockSpec(memory_space=pl.ANY),
            pl.BlockSpec(memory_space=pl.ANY),
        ],
        out_specs=[pl.BlockSpec(memory_space=pltpu.VMEM)] * 2,
        scratch_shapes=[
            pltpu.VMEM((LAYERS, ROWS, COLS), jnp.bfloat16),
            pltpu.VMEM((CAP, ROWS, COLS), f32),
            pltpu.VMEM((8, HALF, COLS), f32),
            pltpu.VMEM((chains, HALF, COLS), f32),
            pltpu.VMEM((CAP, ROWS, COLS), f32),
            pltpu.VMEM((ROWS, COLS), f32),
            pltpu.VMEM((16, PIECE, HALF), f32),
            pltpu.VMEM((2, 7, PIECE, HALF), f32),
            pltpu.VMEM((2, PIECE, HALF), f32),
            pltpu.VMEM((2, 7, PIECE, HALF), f32),
            pltpu.VMEM((2, PIECE, HALF), f32),
            pltpu.VMEM((16, PIECE, HALF), f32),
            pltpu.VMEM((2, ROWS, COLS), f32),
            pltpu.VMEM((OWNERS * CAP, BLOCK, COLS), f32),
            dma((2,)),
            dma((chains,)),
            dma((chains,)),
            dma,
            dma,
            dma((42,)),
            dma((42,)),
            dma((16,)),
            dma((16,)),
            regular,
            regular,
            regular,
            regular,
            regular,
            regular,
        ],
        compiler_params=pltpu.CompilerParams(
            collective_id=0, has_side_effects=True, vmem_limit_bytes=63 * 1024 * 1024
        ),
    )(owner, grad_partial, momentum)


def solution(mesh):
    placed = (P("expert", None, None, "dp"), P("expert", None, "dp"), P())
    return jax.shard_map(
        on_device,
        mesh=mesh,
        in_specs=placed,
        out_specs=(P("expert", None, "dp"), P(None, "expert", "dp")),
        check_vma=False,
    )
```

```python
import functools
import math

import jax
import jax.numpy as jnp
from jax import lax
from jax.experimental import pallas as pl
from jax.experimental.pallas import tpu as pltpu
from jax.sharding import PartitionSpec as P

N = 16384
CAP = 2
OWNERS = 8
LAYERS = 12
ROWS = 256
COLS = 128
HALF = ROWS // 2
BLOCK = ROWS // OWNERS
TILE = ROWS // 16
PIECE = TILE + 1

momentum_rate = 0.95
epsilon = 1e-07
quintic_one = 3.4445
quintic_two = -4.775
quintic_three = 2.0315
update_gain = 0.2

MESH = pl.DeviceIdType.MESH
FAR_FIRST = (4, 3, 5, 2, 6, 1, 7)
STEPS = 4
PARTS = (slice(0, HALF), slice(HALF, ROWS))


def split(value):
    high = value.astype(jnp.bfloat16)
    low = (value - high.astype(jnp.float32)).astype(jnp.bfloat16)
    return high, low


def dot(left, right, dims):
    return lax.dot_general(left, right, (dims, ((), ())), preferred_element_type=jnp.float32)


def product(left, right, dims=((1,), (0,))):
    cross = dot(left[0], right[1], dims) + dot(left[1], right[0], dims)
    return dot(left[0], right[0], dims) + cross


def mod8(value):
    return lax.rem(value + 16, 8)


def kernel(
    owner_hbm,
    grad_hbm,
    momentum_hbm,
    owned_hbm,
    update_hbm,
    owner_ref,
    grad_ref,
    momentum_ref,
    first_ref,
    chain_ref,
    owned_ref,
    field_ref,
    pair_ref,
    base_out_ref,
    base_ref,
    back_out_ref,
    back_ref,
    last_ref,
    gram_ref,
    early_ref,
    early_sum_ref,
    late_ref,
    late_sum_ref,
    whole_ref,
    result_ref,
    rows_ref,
    update_ref,
    load_sem,
    chain_send,
    chain_recv,
    last_recv,
    pair_send,
    pair_recv,
    gram_send,
    gram_recv,
    rows_send,
    rows_recv,
):
    place = lax.axis_index("dp")
    x = lax.axis_index("expert")
    y, z, core = place // 16, lax.rem(place // 2, 8), lax.rem(place, 2)

    def device(y_, z_, core_, x_):
        return ((y_ * 8 + z_) * 2 + core_, x_)

    def signal(sem, target):
        pl.semaphore_signal(sem, inc=1, device_id=target, device_id_type=MESH)

    barrier = pltpu.get_barrier_semaphore()

    for ahead in (1, 7, 2, 6, 3, 5, 4):
        for other in range(2):
            signal(barrier, device(y, z, other, mod8(x + ahead)))
    for ahead in range(1, 8):
        signal(barrier, device(mod8(y + ahead), z, core, x))
        signal(barrier, device(y, mod8(z + ahead), core, x))
    signal(barrier, device(y, z, 1 - core, x))

    load_grad = pltpu.make_async_copy(grad_hbm.at[0], grad_ref, load_sem.at[0])
    load_momentum = pltpu.make_async_copy(momentum_hbm, momentum_ref, load_sem.at[1])
    load_owner = pltpu.make_async_copy(owner_hbm, owner_ref, load_sem.at[2])
    load_owner.start()
    load_grad.start()
    load_momentum.start()

    load_owner.wait()
    owners = [owner_ref[layer] for layer in range(LAYERS)]
    layers = []
    for ahead in range(OWNERS):
        wanted = mod8(x + ahead)
        first = jnp.int32(-1)
        second = jnp.int32(-1)
        for layer in range(LAYERS):
            hit = owners[layer] == wanted
            second = jnp.where(hit & (first >= 0), layer, second)
            first = jnp.where(hit & (first < 0), layer, first)
        layers.append((first, second))

    def share(ahead, slot, part):
        first, second = layers[ahead % 8]
        layer = jnp.where(slot == 0, first, second)
        value = grad_ref[jnp.maximum(layer, 0), PARTS[part], :].astype(jnp.float32)
        return jnp.where(layer >= 0, value, 0.0)

    load_grad.wait()
    pl.semaphore_wait(barrier, 29)

    def length_of(direction, slot, part):
        return 4 - (direction + slot + part) % 2

    def chain_copy(direction, slot, part, step):
        index = direction * 2 + slot
        at = index * STEPS + step
        source = first_ref.at[index] if step == 0 else chain_ref.at[at - 1]
        target = mod8(x + 1) if direction == 0 else mod8(x + 7)
        rows = PARTS[part]
        if step < length_of(direction, slot, part) - 1:
            to_core, into, arrived = core, chain_ref.at[at, rows, :], chain_recv.at[at * 2 + part]
        else:
            to_core, into, arrived = slot, last_ref.at[core, direction, rows, :], last_recv.at[core, direction, part]
        return pltpu.make_async_remote_copy(
            src_ref=source.at[rows, :],
            dst_ref=into,
            send_sem=chain_send.at[at * 2 + part],
            recv_sem=arrived,
            device_id=device(y, z, to_core, target),
            device_id_type=MESH,
        )

    def last_arrival(from_core, direction, part):
        rows = PARTS[part]
        pltpu.make_async_remote_copy(
            src_ref=first_ref.at[0, rows, :],
            dst_ref=last_ref.at[from_core, direction, rows, :],
            send_sem=chain_send.at[part],
            recv_sem=last_recv.at[from_core, direction, part],
            device_id=device(y, z, core, mod8(x + 1)),
            device_id_type=MESH,
        ).wait_recv()

    def advance(slot, step, parts=(0, 1)):
        for part in parts:
            for direction in (1, 0):
                length = length_of(direction, slot, part)
                if step >= length:
                    continue
                ahead = length - step if direction == 0 else step - length
                index = direction * 2 + slot
                if step == 0:
                    first_ref[index, PARTS[part], :] = share(ahead, slot, part)
                else:
                    chain_copy(direction, slot, part, step - 1).wait_recv()
                    at = index * STEPS + step - 1
                    chain_ref[at, PARTS[part], :] = chain_ref[at, PARTS[part], :] + share(ahead, slot, part)
                copy = chain_copy(direction, slot, part, step)
                copy.start()
                started.append(copy)

    def to_sibling(source, target, index):
        return pltpu.make_async_remote_copy(
            src_ref=source,
            dst_ref=target,
            send_sem=pair_send.at[index],
            recv_sem=pair_recv.at[index],
            device_id=device(y, z, 1 - core, x),
            device_id_type=MESH,
        )

    base = to_sibling(base_out_ref, base_ref, 0)
    back = to_sibling(back_out_ref, back_ref, 1)

    def send_base():
        for part in range(2):
            rows = PARTS[part]
            own = share(0, 1 - core, part)
            fresh = momentum_rate * momentum_ref[1 - core, rows, :] + own
            base_out_ref[rows, :] = own + momentum_rate * fresh
        base.start()

    def finish():
        base.wait_recv()
        for part in range(2):
            rows = PARTS[part]
            for from_core in range(2):
                for direction in range(2):
                    last_arrival(from_core, direction, part)
            chains = last_ref[core, 0, rows, :] + last_ref[core, 1, rows, :]
            total = share(0, core, part) + chains
            fresh = momentum_rate * momentum_ref[core, rows, :] + total
            owned_ref[core, rows, :] = total
            field_ref[rows, :] = total + momentum_rate * fresh
            chains = last_ref[1 - core, 0, rows, :] + last_ref[1 - core, 1, rows, :]
            back_out_ref[rows, :] = chains
            pair_ref[rows, :] = base_ref[rows, :] + (1.0 + momentum_rate) * chains

    row = lax.broadcasted_iota(jnp.int32, (HALF, HALF), 0)
    column = lax.broadcasted_iota(jnp.int32, (HALF, HALF), 1)

    def along(axis, ahead):
        return device(mod8(y + ahead), z, core, x) if axis == 0 else device(y, mod8(z + ahead), core, x)

    where = (y, z)

    def gram_copy(stage, order, ahead):
        axis = 1 - order if stage == 1 else order
        if stage == 0:
            source, target = gram_ref.at[order * 8 + mod8(where[order] + ahead)], early_ref.at[order, ahead - 1]
        elif stage == 1:
            source, target = early_sum_ref.at[order], late_ref.at[order, ahead - 1]
        else:
            source, target = late_sum_ref.at[order], whole_ref.at[order * 8 + where[order]]
        index = (stage * 2 + order) * 7 + ahead - 1
        return pltpu.make_async_remote_copy(
            src_ref=source,
            dst_ref=target,
            send_sem=gram_send.at[index],
            recv_sem=gram_recv.at[index],
            device_id=along(axis, ahead),
            device_id_type=MESH,
        )

    def gram_arrival(stage, order, ahead):
        if stage < 2:
            gram_copy(stage, order, ahead).wait_recv()
            return
        index = (stage * 2 + order) * 7 + ahead - 1
        pltpu.make_async_remote_copy(
            src_ref=late_sum_ref.at[order],
            dst_ref=whole_ref.at[order * 8 + mod8(where[order] - ahead)],
            send_sem=gram_send.at[index],
            recv_sem=gram_recv.at[index],
            device_id=along(order, ahead),
            device_id_type=MESH,
        ).wait_recv()

    def start_gram():
        rows_rows = ((1,), (1,))
        mine = split(field_ref[...])
        gram = product(mine, mine, rows_rows)
        other = split(pair_ref[...])
        gram = gram + product(other, other, rows_rows)
        corner, side, rest = gram[:HALF, :HALF], gram[:HALF, HALF:], gram[HALF:, HALF:]
        folded = jnp.where(row >= column, corner, rest)
        edge = jnp.sum(jnp.where(row == column, rest, 0.0), axis=0, keepdims=True)
        gram_ref[:, :TILE, :] = jnp.concatenate([side, folded], axis=0).reshape(16, TILE, HALF)
        piece = lax.broadcasted_iota(jnp.int32, (16, HALF), 0)
        lane = lax.broadcasted_iota(jnp.int32, (16, HALF), 1)
        gram_ref[:, TILE, :] = jnp.where(lane // 8 == piece, edge, 0.0)
        start_stage(0)

    def start_stage(stage):
        for ahead in FAR_FIRST:
            for order in range(2):
                gram_copy(stage, order, ahead).start()

    started = [base, back]
    for step in range(STEPS):
        for slot in range(CAP):
            advance(slot, step)
        if step == 0:
            load_momentum.wait()
            send_base()
    finish()
    start_gram()
    back.start()
    back.wait_recv()
    for part in range(2):
        rows = PARTS[part]
        owned_ref[1 - core, rows, :] = share(0, 1 - core, part) + back_ref[rows, :]
    store = pltpu.make_async_copy(owned_ref, owned_hbm, load_sem.at[3])
    store.start()

    for stage in range(3):
        for order in range(2):
            for ahead in range(1, 8):
                started.append(gram_copy(stage, order, ahead))

    for order in range(2):
        total = gram_ref[order * 8 + where[order]]
        for ahead in range(1, 8):
            gram_arrival(0, order, ahead)
            total = total + early_ref[order, ahead - 1]
        early_sum_ref[order] = total
    start_stage(1)
    for order in range(2):
        total = early_sum_ref[order]
        for ahead in range(1, 8):
            gram_arrival(1, order, ahead)
            total = total + late_ref[order, ahead - 1]
        late_sum_ref[order] = total
        whole_ref[order * 8 + where[order]] = total
    start_stage(2)
    for order in range(2):
        for ahead in range(1, 8):
            gram_arrival(2, order, ahead)

    blocks = whole_ref[:, :TILE, :].reshape(2 * HALF, HALF)
    edge = jnp.sum(whole_ref[:, TILE, :], axis=0, keepdims=True)
    side, folded = blocks[:HALF], blocks[HALF:]
    flipped = folded.T
    corner = jnp.where(row >= column, folded, flipped)
    rest = jnp.where(row < column, folded, jnp.where(row == column, edge, flipped))
    squares = jnp.sum(jnp.where(row == column, corner + rest, 0.0))
    scale = 1.0 / (jnp.sqrt(jnp.full((1, 1), squares, jnp.float32)) + epsilon)
    gram = jnp.concatenate(
        [jnp.concatenate([corner, side], axis=1), jnp.concatenate([side.T, rest], axis=1)], axis=0
    )
    gram = gram * (scale * scale)
    field = jnp.concatenate([field_ref[...], pair_ref[...]], axis=1) * scale

    for step in range(2):
        gram_split = split(gram)
        square = product(gram_split, gram_split)
        square_split = split(square)
        cube = product(gram_split, square_split)
        mixer = quintic_two * gram + quintic_three * square
        mixed = quintic_one * gram + quintic_two * square + quintic_three * cube
        mixer_split = split(mixer)
        field = quintic_one * field + product(mixer_split, split(field))
        gram = quintic_one * mixed + product(split(mixed), mixer_split)
    gram_split = split(gram)
    bent = product(gram_split, split(field))
    twice = product(gram_split, split(bent))
    result = quintic_one * field + quintic_two * bent + quintic_three * twice

    result_ref[0] = result[:, :COLS]
    result_ref[1] = result[:, COLS:]

    def rows_copy(ahead, other_core):
        target = mod8(x + ahead)
        index = other_core * 8 + ahead
        return pltpu.make_async_remote_copy(
            src_ref=result_ref.at[other_core, pl.ds(pl.multiple_of(target * BLOCK, BLOCK), BLOCK), :],
            dst_ref=rows_ref.at[x * 2 + core],
            send_sem=rows_send.at[index],
            recv_sem=rows_recv.at[index],
            device_id=device(y, z, core if other_core == 0 else 1 - core, target),
            device_id_type=MESH,
        )

    def rows_arrival(ahead, other_core):
        source = mod8(x - ahead)
        from_core = core if other_core == 0 else 1 - core
        index = other_core * 8 + ahead
        pltpu.make_async_remote_copy(
            src_ref=result_ref.at[other_core, pl.ds(0, BLOCK), :],
            dst_ref=rows_ref.at[source * 2 + from_core],
            send_sem=rows_send.at[index],
            recv_sem=rows_recv.at[index],
            device_id=device(y, z, from_core, mod8(x + ahead)),
            device_id_type=MESH,
        ).wait_recv()

    partners = [(ahead, other_core) for ahead in FAR_FIRST for other_core in range(2)] + [(0, 1)]
    for ahead, other_core in partners:
        copy = rows_copy(ahead, other_core)
        copy.start()
        started.append(copy)
    rows_ref[x * 2 + core] = result_ref[0, pl.ds(pl.multiple_of(x * BLOCK, BLOCK), BLOCK), :]
    slots = []
    for layer in range(LAYERS):
        rank = jnp.int32(0)
        for before in range(layer):
            rank = rank + (owners[before] == owners[layer]).astype(jnp.int32)
        slots.append(owners[layer] * CAP + rank)
    for ahead, other_core in partners:
        rows_arrival(ahead, other_core)
    for layer in range(LAYERS):
        update_ref[layer] = rows_ref[slots[layer]]
    store_update = pltpu.make_async_copy(update_ref, update_hbm, load_sem.at[4])
    store_update.start()
    for copy in started:
        copy.wait_send()
    store.wait()
    store_update.wait()


def on_device(grad_partial, momentum, owner):
    f32 = jnp.float32
    chains = 8 * STEPS
    dma = pltpu.SemaphoreType.DMA
    shapes = (
        jax.ShapeDtypeStruct((CAP, ROWS, COLS), f32),
        jax.ShapeDtypeStruct((LAYERS, BLOCK, COLS), f32),
    )
    anywhere = pl.BlockSpec(memory_space=pl.ANY)
    owned, update = pl.pallas_call(
        kernel,
        out_shape=shapes,
        in_specs=[anywhere] * 3,
        out_specs=[anywhere] * 2,
        scratch_shapes=[
            pltpu.SMEM((LAYERS,), jnp.int32),
            pltpu.VMEM((LAYERS, ROWS, COLS), jnp.bfloat16),
            pltpu.VMEM((CAP, ROWS, COLS), f32),
            pltpu.VMEM((4, ROWS, COLS), f32),
            pltpu.VMEM((4 * STEPS, ROWS, COLS), f32),
            pltpu.VMEM((CAP, ROWS, COLS), f32),
            pltpu.VMEM((ROWS, COLS), f32),
            pltpu.VMEM((ROWS, COLS), f32),
            pltpu.VMEM((ROWS, COLS), f32),
            pltpu.VMEM((ROWS, COLS), f32),
            pltpu.VMEM((ROWS, COLS), f32),
            pltpu.VMEM((ROWS, COLS), f32),
            pltpu.VMEM((2, 2, ROWS, COLS), f32),
            pltpu.VMEM((16, PIECE, HALF), f32),
            pltpu.VMEM((2, 7, PIECE, HALF), f32),
            pltpu.VMEM((2, PIECE, HALF), f32),
            pltpu.VMEM((2, 7, PIECE, HALF), f32),
            pltpu.VMEM((2, PIECE, HALF), f32),
            pltpu.VMEM((16, PIECE, HALF), f32),
            pltpu.VMEM((2, ROWS, COLS), f32),
            pltpu.VMEM((OWNERS * CAP, BLOCK, COLS), f32),
            pltpu.VMEM((LAYERS, BLOCK, COLS), f32),
            dma((5,)),
            dma((chains,)),
            dma((chains,)),
            dma((2, 2, 2)),
            dma((2,)),
            dma((2,)),
            dma((42,)),
            dma((42,)),
            dma((16,)),
            dma((16,)),
        ],
        compiler_params=pltpu.CompilerParams(
            collective_id=0, has_side_effects=True, vmem_limit_bytes=63 * 1024 * 1024
        ),
    )(owner, grad_partial, momentum)
    return momentum_rate * momentum + owned, update_gain * math.sqrt(N) * update


def solution(mesh):
    placed = (P("expert", None, None, "dp"), P("expert", None, "dp"), P())
    return jax.shard_map(
        on_device,
        mesh=mesh,
        in_specs=placed,
        out_specs=(P("expert", None, "dp"), P(None, "expert", "dp")),
        check_vma=False,
    )
```

```python
import functools
import math

import jax
import jax.numpy as jnp
from jax import lax
from jax.experimental import pallas as pl
from jax.experimental.pallas import tpu as pltpu
from jax.sharding import PartitionSpec as P

N = 16384
CAP = 2
OWNERS = 8
LAYERS = 12
ROWS = 256
COLS = 128
HALF = ROWS // 2
BLOCK = ROWS // OWNERS
TILE = ROWS // 16
PIECE = TILE + 1

momentum_rate = 0.95
epsilon = 1e-07
quintic_one = 3.4445
quintic_two = -4.775
quintic_three = 2.0315
update_gain = 0.2

MESH = pl.DeviceIdType.MESH
FAR_FIRST = (4, 3, 5, 2, 6, 1, 7)
STEPS = 4
PARTS = (slice(0, HALF), slice(HALF, ROWS))


def split(value):
    high = value.astype(jnp.bfloat16)
    low = (value - high.astype(jnp.float32)).astype(jnp.bfloat16)
    return high, low


def dot(left, right, dims):
    return lax.dot_general(left, right, (dims, ((), ())), preferred_element_type=jnp.float32)


def product(left, right, dims=((1,), (0,))):
    cross = dot(left[0], right[1], dims) + dot(left[1], right[0], dims)
    return dot(left[0], right[0], dims) + cross


def mod8(value):
    return lax.rem(value + 16, 8)


def kernel(
    owner_hbm,
    grad_hbm,
    momentum_hbm,
    new_momentum_hbm,
    rows_ref,
    owner_ref,
    grad_ref,
    momentum_ref,
    first_ref,
    chain_ref,
    fresh_ref,
    field_ref,
    pair_ref,
    base_out_ref,
    base_ref,
    back_out_ref,
    back_ref,
    last_ref,
    gram_ref,
    early_ref,
    early_sum_ref,
    late_ref,
    late_sum_ref,
    whole_ref,
    result_ref,
    load_sem,
    chain_send,
    chain_recv,
    last_recv,
    pair_send,
    pair_recv,
    gram_send,
    gram_recv,
    rows_send,
    rows_recv,
):
    place = lax.axis_index("dp")
    x = lax.axis_index("expert")
    y, z, core = place // 16, lax.rem(place // 2, 8), lax.rem(place, 2)

    def device(y_, z_, core_, x_):
        return ((y_ * 8 + z_) * 2 + core_, x_)

    def signal(sem, target):
        pl.semaphore_signal(sem, inc=1, device_id=target, device_id_type=MESH)

    barrier = pltpu.get_barrier_semaphore()

    for ahead in (1, 7, 2, 6, 3, 5, 4):
        for other in range(2):
            signal(barrier, device(y, z, other, mod8(x + ahead)))
    for ahead in range(1, 8):
        signal(barrier, device(mod8(y + ahead), z, core, x))
        signal(barrier, device(y, mod8(z + ahead), core, x))
    signal(barrier, device(y, z, 1 - core, x))

    load_grad = pltpu.make_async_copy(grad_hbm.at[0], grad_ref, load_sem.at[0])
    load_momentum = pltpu.make_async_copy(momentum_hbm, momentum_ref, load_sem.at[1])
    load_owner = pltpu.make_async_copy(owner_hbm, owner_ref, load_sem.at[2])
    load_owner.start()
    load_grad.start()
    load_momentum.start()

    load_owner.wait()
    owners = [owner_ref[layer] for layer in range(LAYERS)]
    layers = []
    for ahead in range(OWNERS):
        wanted = mod8(x + ahead)
        first = jnp.int32(-1)
        second = jnp.int32(-1)
        for layer in range(LAYERS):
            hit = owners[layer] == wanted
            second = jnp.where(hit & (first >= 0), layer, second)
            first = jnp.where(hit & (first < 0), layer, first)
        layers.append((first, second))

    def share(ahead, slot, part):
        first, second = layers[ahead % 8]
        layer = jnp.where(slot == 0, first, second)
        value = grad_ref[jnp.maximum(layer, 0), PARTS[part], :].astype(jnp.float32)
        return jnp.where(layer >= 0, value, 0.0)

    load_grad.wait()
    pl.semaphore_wait(barrier, 29)

    def length_of(direction, slot, part):
        return 4 - (direction + slot + part) % 2

    def chain_copy(direction, slot, part, step):
        index = direction * 2 + slot
        at = index * STEPS + step
        source = first_ref.at[index] if step == 0 else chain_ref.at[at - 1]
        target = mod8(x + 1) if direction == 0 else mod8(x + 7)
        rows = PARTS[part]
        if step < length_of(direction, slot, part) - 1:
            to_core, into, arrived = core, chain_ref.at[at, rows, :], chain_recv.at[at * 2 + part]
        else:
            to_core, into, arrived = slot, last_ref.at[core, direction, rows, :], last_recv.at[core, direction, part]
        return pltpu.make_async_remote_copy(
            src_ref=source.at[rows, :],
            dst_ref=into,
            send_sem=chain_send.at[at * 2 + part],
            recv_sem=arrived,
            device_id=device(y, z, to_core, target),
            device_id_type=MESH,
        )

    def last_arrival(from_core, direction, part):
        rows = PARTS[part]
        pltpu.make_async_remote_copy(
            src_ref=first_ref.at[0, rows, :],
            dst_ref=last_ref.at[from_core, direction, rows, :],
            send_sem=chain_send.at[part],
            recv_sem=last_recv.at[from_core, direction, part],
            device_id=device(y, z, core, mod8(x + 1)),
            device_id_type=MESH,
        ).wait_recv()

    def advance(slot, step, parts=(0, 1)):
        for part in parts:
            for direction in (1, 0):
                length = length_of(direction, slot, part)
                if step >= length:
                    continue
                ahead = length - step if direction == 0 else step - length
                index = direction * 2 + slot
                if step == 0:
                    first_ref[index, PARTS[part], :] = share(ahead, slot, part)
                else:
                    chain_copy(direction, slot, part, step - 1).wait_recv()
                    at = index * STEPS + step - 1
                    chain_ref[at, PARTS[part], :] = chain_ref[at, PARTS[part], :] + share(ahead, slot, part)
                copy = chain_copy(direction, slot, part, step)
                copy.start()
                started.append(copy)

    def to_sibling(source, target, index):
        return pltpu.make_async_remote_copy(
            src_ref=source,
            dst_ref=target,
            send_sem=pair_send.at[index],
            recv_sem=pair_recv.at[index],
            device_id=device(y, z, 1 - core, x),
            device_id_type=MESH,
        )

    base = to_sibling(base_out_ref, base_ref, 0)
    back = to_sibling(back_out_ref, back_ref, 1)

    def send_base():
        for part in range(2):
            rows = PARTS[part]
            own = share(0, 1 - core, part)
            fresh = momentum_rate * momentum_ref[1 - core, rows, :] + own
            base_out_ref[rows, :] = own + momentum_rate * fresh
        base.start()

    def finish():
        base.wait_recv()
        for part in range(2):
            rows = PARTS[part]
            for from_core in range(2):
                for direction in range(2):
                    last_arrival(from_core, direction, part)
            chains = last_ref[core, 0, rows, :] + last_ref[core, 1, rows, :]
            total = share(0, core, part) + chains
            fresh = momentum_rate * momentum_ref[core, rows, :] + total
            fresh_ref[core, rows, :] = fresh
            field_ref[rows, :] = total + momentum_rate * fresh
            chains = last_ref[1 - core, 0, rows, :] + last_ref[1 - core, 1, rows, :]
            back_out_ref[rows, :] = chains
            pair_ref[rows, :] = base_ref[rows, :] + (1.0 + momentum_rate) * chains

    row = lax.broadcasted_iota(jnp.int32, (HALF, HALF), 0)
    column = lax.broadcasted_iota(jnp.int32, (HALF, HALF), 1)

    def along(axis, ahead):
        return device(mod8(y + ahead), z, core, x) if axis == 0 else device(y, mod8(z + ahead), core, x)

    where = (y, z)

    def gram_copy(stage, order, ahead):
        axis = 1 - order if stage == 1 else order
        if stage == 0:
            source, target = gram_ref.at[order * 8 + mod8(where[order] + ahead)], early_ref.at[order, ahead - 1]
        elif stage == 1:
            source, target = early_sum_ref.at[order], late_ref.at[order, ahead - 1]
        else:
            source, target = late_sum_ref.at[order], whole_ref.at[order * 8 + where[order]]
        index = (stage * 2 + order) * 7 + ahead - 1
        return pltpu.make_async_remote_copy(
            src_ref=source,
            dst_ref=target,
            send_sem=gram_send.at[index],
            recv_sem=gram_recv.at[index],
            device_id=along(axis, ahead),
            device_id_type=MESH,
        )

    def gram_arrival(stage, order, ahead):
        if stage < 2:
            gram_copy(stage, order, ahead).wait_recv()
            return
        index = (stage * 2 + order) * 7 + ahead - 1
        pltpu.make_async_remote_copy(
            src_ref=late_sum_ref.at[order],
            dst_ref=whole_ref.at[order * 8 + mod8(where[order] - ahead)],
            send_sem=gram_send.at[index],
            recv_sem=gram_recv.at[index],
            device_id=along(order, ahead),
            device_id_type=MESH,
        ).wait_recv()

    def start_gram():
        rows_rows = ((1,), (1,))
        mine = split(field_ref[...])
        gram = product(mine, mine, rows_rows)
        other = split(pair_ref[...])
        gram = gram + product(other, other, rows_rows)
        corner, side, rest = gram[:HALF, :HALF], gram[:HALF, HALF:], gram[HALF:, HALF:]
        folded = jnp.where(row >= column, corner, rest)
        edge = jnp.sum(jnp.where(row == column, rest, 0.0), axis=0, keepdims=True)
        gram_ref[:, :TILE, :] = jnp.concatenate([side, folded], axis=0).reshape(16, TILE, HALF)
        piece = lax.broadcasted_iota(jnp.int32, (16, HALF), 0)
        lane = lax.broadcasted_iota(jnp.int32, (16, HALF), 1)
        gram_ref[:, TILE, :] = jnp.where(lane // 8 == piece, edge, 0.0)
        start_stage(0)

    def start_stage(stage):
        for ahead in FAR_FIRST:
            for order in range(2):
                gram_copy(stage, order, ahead).start()

    started = [base, back]
    for step in range(STEPS):
        for slot in range(CAP):
            advance(slot, step)
        if step == 0:
            load_momentum.wait()
            send_base()
    finish()
    start_gram()
    back.start()
    back.wait_recv()
    for part in range(2):
        rows = PARTS[part]
        total = share(0, 1 - core, part) + back_ref[rows, :]
        fresh_ref[1 - core, rows, :] = momentum_rate * momentum_ref[1 - core, rows, :] + total
    store = pltpu.make_async_copy(fresh_ref, new_momentum_hbm, load_sem.at[3])
    store.start()

    for stage in range(3):
        for order in range(2):
            for ahead in range(1, 8):
                started.append(gram_copy(stage, order, ahead))

    for order in range(2):
        total = gram_ref[order * 8 + where[order]]
        for ahead in range(1, 8):
            gram_arrival(0, order, ahead)
            total = total + early_ref[order, ahead - 1]
        early_sum_ref[order] = total
    start_stage(1)
    for order in range(2):
        total = early_sum_ref[order]
        for ahead in range(1, 8):
            gram_arrival(1, order, ahead)
            total = total + late_ref[order, ahead - 1]
        late_sum_ref[order] = total
        whole_ref[order * 8 + where[order]] = total
    start_stage(2)
    for order in range(2):
        for ahead in range(1, 8):
            gram_arrival(2, order, ahead)

    blocks = whole_ref[:, :TILE, :].reshape(2 * HALF, HALF)
    edge = jnp.sum(whole_ref[:, TILE, :], axis=0, keepdims=True)
    side, folded = blocks[:HALF], blocks[HALF:]
    flipped = folded.T
    corner = jnp.where(row >= column, folded, flipped)
    rest = jnp.where(row < column, folded, jnp.where(row == column, edge, flipped))
    squares = jnp.sum(jnp.where(row == column, corner + rest, 0.0))
    scale = 1.0 / (jnp.sqrt(jnp.full((1, 1), squares, jnp.float32)) + epsilon)
    gram = jnp.concatenate(
        [jnp.concatenate([corner, side], axis=1), jnp.concatenate([side.T, rest], axis=1)], axis=0
    )
    gram = gram * (scale * scale)
    field = jnp.concatenate([field_ref[...], pair_ref[...]], axis=1) * scale

    for step in range(2):
        gram_split = split(gram)
        square = product(gram_split, gram_split)
        square_split = split(square)
        cube = product(gram_split, square_split)
        mixer = quintic_two * gram + quintic_three * square
        mixed = quintic_one * gram + quintic_two * square + quintic_three * cube
        mixer_split = split(mixer)
        field = quintic_one * field + product(mixer_split, split(field))
        gram = quintic_one * mixed + product(split(mixed), mixer_split)
    gram_split = split(gram)
    bent = product(gram_split, split(field))
    twice = product(gram_split, split(bent))
    gain = update_gain * math.sqrt(N)
    result = (gain * quintic_one) * field + (gain * quintic_two) * bent + (gain * quintic_three) * twice

    result_ref[0] = result[:, :COLS]
    result_ref[1] = result[:, COLS:]

    def rows_copy(ahead, other_core):
        target = mod8(x + ahead)
        index = other_core * 8 + ahead
        return pltpu.make_async_remote_copy(
            src_ref=result_ref.at[other_core, pl.ds(pl.multiple_of(target * BLOCK, BLOCK), BLOCK), :],
            dst_ref=rows_ref.at[x * 2 + core],
            send_sem=rows_send.at[index],
            recv_sem=rows_recv.at[index],
            device_id=device(y, z, core if other_core == 0 else 1 - core, target),
            device_id_type=MESH,
        )

    def rows_arrival(ahead, other_core):
        source = mod8(x - ahead)
        from_core = core if other_core == 0 else 1 - core
        index = other_core * 8 + ahead
        pltpu.make_async_remote_copy(
            src_ref=result_ref.at[other_core, pl.ds(0, BLOCK), :],
            dst_ref=rows_ref.at[source * 2 + from_core],
            send_sem=rows_send.at[index],
            recv_sem=rows_recv.at[index],
            device_id=device(y, z, from_core, mod8(x + ahead)),
            device_id_type=MESH,
        ).wait_recv()

    partners = [(ahead, other_core) for ahead in FAR_FIRST for other_core in range(2)] + [(0, 1)]
    for ahead, other_core in partners:
        copy = rows_copy(ahead, other_core)
        copy.start()
        started.append(copy)
    keep = pltpu.make_async_copy(
        result_ref.at[0, pl.ds(pl.multiple_of(x * BLOCK, BLOCK), BLOCK), :], rows_ref.at[x * 2 + core], load_sem.at[4]
    )
    keep.start()
    for ahead, other_core in partners:
        rows_arrival(ahead, other_core)
    for copy in started:
        copy.wait_send()
    store.wait()
    keep.wait()


def hand_over(
    owner_hbm, fresh_hbm, rows_hbm, new_momentum_hbm, update_hbm, owner_ref, fresh_ref, rows_ref, update_ref, sems
):
    load_rows = pltpu.make_async_copy(rows_hbm, rows_ref, sems.at[0])
    load_fresh = pltpu.make_async_copy(fresh_hbm, fresh_ref, sems.at[1])
    load_owner = pltpu.make_async_copy(owner_hbm, owner_ref, sems.at[4])
    load_owner.start()
    load_rows.start()
    load_fresh.start()
    load_owner.wait()
    owners = [owner_ref[layer] for layer in range(LAYERS)]
    slots = []
    for layer in range(LAYERS):
        rank = jnp.int32(0)
        for before in range(layer):
            rank = rank + (owners[before] == owners[layer]).astype(jnp.int32)
        slots.append(owners[layer] * CAP + rank)
    load_rows.wait()
    for layer in range(LAYERS):
        update_ref[layer] = rows_ref[slots[layer]]
    store_update = pltpu.make_async_copy(update_ref, update_hbm, sems.at[2])
    store_update.start()
    load_fresh.wait()
    store_fresh = pltpu.make_async_copy(fresh_ref, new_momentum_hbm, sems.at[3])
    store_fresh.start()
    store_update.wait()
    store_fresh.wait()


def on_device(grad_partial, momentum, owner):
    f32 = jnp.float32
    chains = 8 * STEPS
    dma = pltpu.SemaphoreType.DMA
    fresh = jax.ShapeDtypeStruct((CAP, ROWS, COLS), f32)
    rows = jax.ShapeDtypeStruct((OWNERS * CAP, BLOCK, COLS), f32)
    update = jax.ShapeDtypeStruct((LAYERS, BLOCK, COLS), f32)
    anywhere = pl.BlockSpec(memory_space=pl.ANY)
    held = pl.pallas_call(
        kernel,
        out_shape=(fresh, rows),
        in_specs=[anywhere] * 3,
        out_specs=[anywhere] * 2,
        scratch_shapes=[
            pltpu.SMEM((LAYERS,), jnp.int32),
            pltpu.VMEM((LAYERS, ROWS, COLS), jnp.bfloat16),
            pltpu.VMEM((CAP, ROWS, COLS), f32),
            pltpu.VMEM((4, ROWS, COLS), f32),
            pltpu.VMEM((4 * STEPS, ROWS, COLS), f32),
            pltpu.VMEM((CAP, ROWS, COLS), f32),
            pltpu.VMEM((ROWS, COLS), f32),
            pltpu.VMEM((ROWS, COLS), f32),
            pltpu.VMEM((ROWS, COLS), f32),
            pltpu.VMEM((ROWS, COLS), f32),
            pltpu.VMEM((ROWS, COLS), f32),
            pltpu.VMEM((ROWS, COLS), f32),
            pltpu.VMEM((2, 2, ROWS, COLS), f32),
            pltpu.VMEM((16, PIECE, HALF), f32),
            pltpu.VMEM((2, 7, PIECE, HALF), f32),
            pltpu.VMEM((2, PIECE, HALF), f32),
            pltpu.VMEM((2, 7, PIECE, HALF), f32),
            pltpu.VMEM((2, PIECE, HALF), f32),
            pltpu.VMEM((16, PIECE, HALF), f32),
            pltpu.VMEM((2, ROWS, COLS), f32),
            dma((5,)),
            dma((chains,)),
            dma((chains,)),
            dma((2, 2, 2)),
            dma((2,)),
            dma((2,)),
            dma((42,)),
            dma((42,)),
            dma((16,)),
            dma((16,)),
        ],
        compiler_params=pltpu.CompilerParams(
            collective_id=0, has_side_effects=True, vmem_limit_bytes=63 * 1024 * 1024
        ),
    )(owner, grad_partial, momentum)
    return pl.pallas_call(
        hand_over,
        out_shape=(fresh, update),
        in_specs=[anywhere] * 3,
        out_specs=[anywhere] * 2,
        scratch_shapes=[
            pltpu.SMEM((LAYERS,), jnp.int32),
            pltpu.VMEM((CAP, ROWS, COLS), f32),
            pltpu.VMEM((OWNERS * CAP, BLOCK, COLS), f32),
            pltpu.VMEM((LAYERS, BLOCK, COLS), f32),
            dma((5,)),
        ],
        compiler_params=pltpu.CompilerParams(vmem_limit_bytes=63 * 1024 * 1024),
    )(owner, *held)


def solution(mesh):
    placed = (P("expert", None, None, "dp"), P("expert", None, "dp"), P())
    return jax.shard_map(
        on_device,
        mesh=mesh,
        in_specs=placed,
        out_specs=(P("expert", None, "dp"), P(None, "expert", "dp")),
        check_vma=False,
    )
```

```python
import functools
import math

import jax
import jax.numpy as jnp
from jax import lax
from jax.experimental import pallas as pl
from jax.experimental.pallas import tpu as pltpu
from jax.sharding import PartitionSpec as P

N = 16384
CAP = 2
OWNERS = 8
LAYERS = 12
ROWS = 256
COLS = 128
HALF = ROWS // 2
BLOCK = ROWS // OWNERS
TILE = ROWS // 16
PIECE = TILE + 1

momentum_rate = 0.95
epsilon = 1e-07
quintic_one = 3.4445
quintic_two = -4.775
quintic_three = 2.0315
update_gain = 0.2

MESH = pl.DeviceIdType.MESH
FAR_FIRST = (4, 3, 5, 2, 6, 1, 7)
STEPS = 4
PARTS = (slice(0, HALF), slice(HALF, ROWS))


def split(value):
    high = value.astype(jnp.bfloat16)
    low = (value - high.astype(jnp.float32)).astype(jnp.bfloat16)
    return high, low


def dot(left, right, dims):
    return lax.dot_general(left, right, (dims, ((), ())), preferred_element_type=jnp.float32)


def product(left, right, dims=((1,), (0,))):
    cross = dot(left[0], right[1], dims) + dot(left[1], right[0], dims)
    return dot(left[0], right[0], dims) + cross


def mod8(value):
    return lax.rem(value + 16, 8)


def kernel(
    owner_hbm,
    grad_hbm,
    momentum_hbm,
    new_momentum_hbm,
    rows_ref,
    owner_ref,
    grad_ref,
    momentum_ref,
    first_ref,
    chain_ref,
    fresh_ref,
    field_ref,
    pair_ref,
    base_out_ref,
    base_ref,
    back_out_ref,
    back_ref,
    last_ref,
    gram_ref,
    early_ref,
    early_sum_ref,
    late_ref,
    late_sum_ref,
    whole_ref,
    result_ref,
    load_sem,
    chain_send,
    chain_recv,
    last_recv,
    pair_send,
    pair_recv,
    gram_send,
    gram_recv,
    rows_send,
    rows_recv,
):
    place = lax.axis_index("dp")
    x = lax.axis_index("expert")
    y, z, core = place // 16, lax.rem(place // 2, 8), lax.rem(place, 2)

    def device(y_, z_, core_, x_):
        return ((y_ * 8 + z_) * 2 + core_, x_)

    def signal(sem, target):
        pl.semaphore_signal(sem, inc=1, device_id=target, device_id_type=MESH)

    barrier = pltpu.get_barrier_semaphore()

    for ahead in (1, 7, 2, 6, 3, 5, 4):
        for other in range(2):
            signal(barrier, device(y, z, other, mod8(x + ahead)))
    for ahead in range(1, 8):
        signal(barrier, device(mod8(y + ahead), z, core, x))
        signal(barrier, device(y, mod8(z + ahead), core, x))
    signal(barrier, device(y, z, 1 - core, x))

    load_grad = pltpu.make_async_copy(grad_hbm.at[0], grad_ref, load_sem.at[0])
    load_momentum = pltpu.make_async_copy(momentum_hbm, momentum_ref, load_sem.at[1])
    load_owner = pltpu.make_async_copy(owner_hbm, owner_ref, load_sem.at[2])
    load_owner.start()
    load_grad.start()
    load_momentum.start()

    load_owner.wait()
    owners = [owner_ref[layer] for layer in range(LAYERS)]
    layers = []
    for ahead in range(OWNERS):
        wanted = mod8(x + ahead)
        first = jnp.int32(-1)
        second = jnp.int32(-1)
        for layer in range(LAYERS):
            hit = owners[layer] == wanted
            second = jnp.where(hit & (first >= 0), layer, second)
            first = jnp.where(hit & (first < 0), layer, first)
        layers.append((first, second))

    def share(ahead, slot, part):
        first, second = layers[ahead % 8]
        layer = jnp.where(slot == 0, first, second)
        value = grad_ref[jnp.maximum(layer, 0), PARTS[part], :].astype(jnp.float32)
        return jnp.where(layer >= 0, value, 0.0)

    load_grad.wait()
    pl.semaphore_wait(barrier, 29)

    def length_of(direction, slot, part):
        return 4 - (direction + slot + part) % 2

    def chain_copy(direction, slot, part, step):
        index = direction * 2 + slot
        at = index * STEPS + step
        source = first_ref.at[index] if step == 0 else chain_ref.at[at - 1]
        target = mod8(x + 1) if direction == 0 else mod8(x + 7)
        rows = PARTS[part]
        if step < length_of(direction, slot, part) - 1:
            to_core, into, arrived = core, chain_ref.at[at, rows, :], chain_recv.at[at * 2 + part]
        else:
            to_core, into, arrived = slot, last_ref.at[core, direction, rows, :], last_recv.at[core, direction, part]
        return pltpu.make_async_remote_copy(
            src_ref=source.at[rows, :],
            dst_ref=into,
            send_sem=chain_send.at[at * 2 + part],
            recv_sem=arrived,
            device_id=device(y, z, to_core, target),
            device_id_type=MESH,
        )

    def last_arrival(from_core, direction, part):
        rows = PARTS[part]
        pltpu.make_async_remote_copy(
            src_ref=first_ref.at[0, rows, :],
            dst_ref=last_ref.at[from_core, direction, rows, :],
            send_sem=chain_send.at[part],
            recv_sem=last_recv.at[from_core, direction, part],
            device_id=device(y, z, core, mod8(x + 1)),
            device_id_type=MESH,
        ).wait_recv()

    def advance(slot, step, parts=(0, 1)):
        for part in parts:
            for direction in (1, 0):
                length = length_of(direction, slot, part)
                if step >= length:
                    continue
                ahead = length - step if direction == 0 else step - length
                index = direction * 2 + slot
                if step == 0:
                    first_ref[index, PARTS[part], :] = share(ahead, slot, part)
                else:
                    chain_copy(direction, slot, part, step - 1).wait_recv()
                    at = index * STEPS + step - 1
                    chain_ref[at, PARTS[part], :] = chain_ref[at, PARTS[part], :] + share(ahead, slot, part)
                copy = chain_copy(direction, slot, part, step)
                copy.start()
                started.append(copy)

    def to_sibling(source, target, index):
        return pltpu.make_async_remote_copy(
            src_ref=source,
            dst_ref=target,
            send_sem=pair_send.at[index],
            recv_sem=pair_recv.at[index],
            device_id=device(y, z, 1 - core, x),
            device_id_type=MESH,
        )

    base = to_sibling(base_out_ref, base_ref, 0)
    back = to_sibling(back_out_ref, back_ref, 1)

    def send_base():
        for part in range(2):
            rows = PARTS[part]
            own = share(0, 1 - core, part)
            fresh = momentum_rate * momentum_ref[1 - core, rows, :] + own
            base_out_ref[rows, :] = own + momentum_rate * fresh
        base.start()

    def finish():
        base.wait_recv()
        for part in range(2):
            rows = PARTS[part]
            for from_core in range(2):
                for direction in range(2):
                    last_arrival(from_core, direction, part)
            chains = last_ref[core, 0, rows, :] + last_ref[core, 1, rows, :]
            total = share(0, core, part) + chains
            fresh = momentum_rate * momentum_ref[core, rows, :] + total
            fresh_ref[core, rows, :] = fresh
            field_ref[rows, :] = total + momentum_rate * fresh
            chains = last_ref[1 - core, 0, rows, :] + last_ref[1 - core, 1, rows, :]
            back_out_ref[rows, :] = chains
            pair_ref[rows, :] = base_ref[rows, :] + (1.0 + momentum_rate) * chains

    row = lax.broadcasted_iota(jnp.int32, (HALF, HALF), 0)
    column = lax.broadcasted_iota(jnp.int32, (HALF, HALF), 1)

    def along(axis, ahead):
        return device(mod8(y + ahead), z, core, x) if axis == 0 else device(y, mod8(z + ahead), core, x)

    where = (y, z)

    def gram_copy(stage, order, ahead):
        axis = 1 - order if stage == 1 else order
        if stage == 0:
            source, target = gram_ref.at[order * 8 + mod8(where[order] + ahead)], early_ref.at[order, ahead - 1]
        elif stage == 1:
            source, target = early_sum_ref.at[order], late_ref.at[order, ahead - 1]
        else:
            source, target = late_sum_ref.at[order], whole_ref.at[order * 8 + where[order]]
        index = (stage * 2 + order) * 7 + ahead - 1
        return pltpu.make_async_remote_copy(
            src_ref=source,
            dst_ref=target,
            send_sem=gram_send.at[index],
            recv_sem=gram_recv.at[index],
            device_id=along(axis, ahead),
            device_id_type=MESH,
        )

    def gram_arrival(stage, order, ahead):
        if stage < 2:
            gram_copy(stage, order, ahead).wait_recv()
            return
        index = (stage * 2 + order) * 7 + ahead - 1
        pltpu.make_async_remote_copy(
            src_ref=late_sum_ref.at[order],
            dst_ref=whole_ref.at[order * 8 + mod8(where[order] - ahead)],
            send_sem=gram_send.at[index],
            recv_sem=gram_recv.at[index],
            device_id=along(order, ahead),
            device_id_type=MESH,
        ).wait_recv()

    def start_gram():
        rows_rows = ((1,), (1,))
        mine = split(field_ref[...])
        gram = product(mine, mine, rows_rows)
        other = split(pair_ref[...])
        gram = gram + product(other, other, rows_rows)
        corner, side, rest = gram[:HALF, :HALF], gram[:HALF, HALF:], gram[HALF:, HALF:]
        folded = jnp.where(row >= column, corner, rest)
        edge = jnp.sum(jnp.where(row == column, rest, 0.0), axis=0, keepdims=True)
        gram_ref[:, :TILE, :] = jnp.concatenate([side, folded], axis=0).reshape(16, TILE, HALF)
        piece = lax.broadcasted_iota(jnp.int32, (16, HALF), 0)
        lane = lax.broadcasted_iota(jnp.int32, (16, HALF), 1)
        gram_ref[:, TILE, :] = jnp.where(lane // 8 == piece, edge, 0.0)
        start_stage(0)

    def start_stage(stage):
        for ahead in FAR_FIRST:
            for order in range(2):
                gram_copy(stage, order, ahead).start()

    started = [base, back]
    for step in range(STEPS):
        for slot in range(CAP):
            advance(slot, step)
        if step == 0:
            load_momentum.wait()
            send_base()
    finish()
    start_gram()
    back.start()
    back.wait_recv()
    for part in range(2):
        rows = PARTS[part]
        total = share(0, 1 - core, part) + back_ref[rows, :]
        fresh_ref[1 - core, rows, :] = momentum_rate * momentum_ref[1 - core, rows, :] + total
    store = pltpu.make_async_copy(fresh_ref, new_momentum_hbm, load_sem.at[3])
    store.start()

    for stage in range(3):
        for order in range(2):
            for ahead in range(1, 8):
                started.append(gram_copy(stage, order, ahead))

    for order in range(2):
        total = gram_ref[order * 8 + where[order]]
        for ahead in range(1, 8):
            gram_arrival(0, order, ahead)
            total = total + early_ref[order, ahead - 1]
        early_sum_ref[order] = total
    start_stage(1)
    for order in range(2):
        total = early_sum_ref[order]
        for ahead in range(1, 8):
            gram_arrival(1, order, ahead)
            total = total + late_ref[order, ahead - 1]
        late_sum_ref[order] = total
        whole_ref[order * 8 + where[order]] = total
    start_stage(2)
    for order in range(2):
        for ahead in range(1, 8):
            gram_arrival(2, order, ahead)

    blocks = whole_ref[:, :TILE, :].reshape(2 * HALF, HALF)
    edge = jnp.sum(whole_ref[:, TILE, :], axis=0, keepdims=True)
    side, folded = blocks[:HALF], blocks[HALF:]
    flipped = folded.T
    corner = jnp.where(row >= column, folded, flipped)
    rest = jnp.where(row < column, folded, jnp.where(row == column, edge, flipped))
    squares = jnp.sum(jnp.where(row == column, corner + rest, 0.0))
    scale = 1.0 / (jnp.sqrt(jnp.full((1, 1), squares, jnp.float32)) + epsilon)
    gram = jnp.concatenate(
        [jnp.concatenate([corner, side], axis=1), jnp.concatenate([side.T, rest], axis=1)], axis=0
    )
    gram = gram * (scale * scale)
    field = jnp.concatenate([field_ref[...], pair_ref[...]], axis=1) * scale

    for step in range(2):
        gram_split = split(gram)
        square = product(gram_split, gram_split)
        square_split = split(square)
        cube = product(gram_split, square_split)
        mixer = quintic_two * gram + quintic_three * square
        mixed = quintic_one * gram + quintic_two * square + quintic_three * cube
        mixer_split = split(mixer)
        field = quintic_one * field + product(mixer_split, split(field))
        gram = quintic_one * mixed + product(split(mixed), mixer_split)
    gram_split = split(gram)
    gain = update_gain * math.sqrt(N)

    def rows_copy(ahead, other_core):
        target = mod8(x + ahead)
        index = other_core * 8 + ahead
        return pltpu.make_async_remote_copy(
            src_ref=result_ref.at[other_core, pl.ds(pl.multiple_of(target * BLOCK, BLOCK), BLOCK), :],
            dst_ref=rows_ref.at[x * 2 + core],
            send_sem=rows_send.at[index],
            recv_sem=rows_recv.at[index],
            device_id=device(y, z, core if other_core == 0 else 1 - core, target),
            device_id_type=MESH,
        )

    def rows_arrival(ahead, other_core):
        source = mod8(x - ahead)
        from_core = core if other_core == 0 else 1 - core
        index = other_core * 8 + ahead
        pltpu.make_async_remote_copy(
            src_ref=result_ref.at[other_core, pl.ds(0, BLOCK), :],
            dst_ref=rows_ref.at[source * 2 + from_core],
            send_sem=rows_send.at[index],
            recv_sem=rows_recv.at[index],
            device_id=device(y, z, from_core, mod8(x + ahead)),
            device_id_type=MESH,
        ).wait_recv()

    for other_core in (1, 0):
        columns = field[:, other_core * COLS : (other_core + 1) * COLS]
        bent = product(gram_split, split(columns))
        twice = product(gram_split, split(bent))
        result_ref[other_core] = gain * (quintic_one * columns + quintic_two * bent + quintic_three * twice)
        for ahead in FAR_FIRST + ((0,) if other_core == 1 else ()):
            copy = rows_copy(ahead, other_core)
            copy.start()
            started.append(copy)
    partners = [(ahead, other_core) for ahead in FAR_FIRST for other_core in range(2)] + [(0, 1)]
    keep = pltpu.make_async_copy(
        result_ref.at[0, pl.ds(pl.multiple_of(x * BLOCK, BLOCK), BLOCK), :], rows_ref.at[x * 2 + core], load_sem.at[4]
    )
    keep.start()
    for ahead, other_core in partners:
        rows_arrival(ahead, other_core)
    for copy in started:
        copy.wait_send()
    store.wait()
    keep.wait()


def hand_over(
    owner_hbm, fresh_hbm, rows_hbm, new_momentum_hbm, update_hbm, owner_ref, fresh_ref, rows_ref, update_ref, sems
):
    load_rows = pltpu.make_async_copy(rows_hbm, rows_ref, sems.at[0])
    load_fresh = pltpu.make_async_copy(fresh_hbm, fresh_ref, sems.at[1])
    load_owner = pltpu.make_async_copy(owner_hbm, owner_ref, sems.at[4])
    load_owner.start()
    load_rows.start()
    load_fresh.start()
    load_owner.wait()
    owners = [owner_ref[layer] for layer in range(LAYERS)]
    slots = []
    for layer in range(LAYERS):
        rank = jnp.int32(0)
        for before in range(layer):
            rank = rank + (owners[before] == owners[layer]).astype(jnp.int32)
        slots.append(owners[layer] * CAP + rank)
    load_rows.wait()
    for layer in range(LAYERS):
        update_ref[layer] = rows_ref[slots[layer]]
    store_update = pltpu.make_async_copy(update_ref, update_hbm, sems.at[2])
    store_update.start()
    load_fresh.wait()
    store_fresh = pltpu.make_async_copy(fresh_ref, new_momentum_hbm, sems.at[3])
    store_fresh.start()
    store_update.wait()
    store_fresh.wait()


def on_device(grad_partial, momentum, owner):
    f32 = jnp.float32
    chains = 8 * STEPS
    dma = pltpu.SemaphoreType.DMA
    fresh = jax.ShapeDtypeStruct((CAP, ROWS, COLS), f32)
    rows = jax.ShapeDtypeStruct((OWNERS * CAP, BLOCK, COLS), f32)
    update = jax.ShapeDtypeStruct((LAYERS, BLOCK, COLS), f32)
    anywhere = pl.BlockSpec(memory_space=pl.ANY)
    held = pl.pallas_call(
        kernel,
        out_shape=(fresh, rows),
        in_specs=[anywhere] * 3,
        out_specs=[anywhere] * 2,
        scratch_shapes=[
            pltpu.SMEM((LAYERS,), jnp.int32),
            pltpu.VMEM((LAYERS, ROWS, COLS), jnp.bfloat16),
            pltpu.VMEM((CAP, ROWS, COLS), f32),
            pltpu.VMEM((4, ROWS, COLS), f32),
            pltpu.VMEM((4 * STEPS, ROWS, COLS), f32),
            pltpu.VMEM((CAP, ROWS, COLS), f32),
            pltpu.VMEM((ROWS, COLS), f32),
            pltpu.VMEM((ROWS, COLS), f32),
            pltpu.VMEM((ROWS, COLS), f32),
            pltpu.VMEM((ROWS, COLS), f32),
            pltpu.VMEM((ROWS, COLS), f32),
            pltpu.VMEM((ROWS, COLS), f32),
            pltpu.VMEM((2, 2, ROWS, COLS), f32),
            pltpu.VMEM((16, PIECE, HALF), f32),
            pltpu.VMEM((2, 7, PIECE, HALF), f32),
            pltpu.VMEM((2, PIECE, HALF), f32),
            pltpu.VMEM((2, 7, PIECE, HALF), f32),
            pltpu.VMEM((2, PIECE, HALF), f32),
            pltpu.VMEM((16, PIECE, HALF), f32),
            pltpu.VMEM((2, ROWS, COLS), f32),
            dma((5,)),
            dma((chains,)),
            dma((chains,)),
            dma((2, 2, 2)),
            dma((2,)),
            dma((2,)),
            dma((42,)),
            dma((42,)),
            dma((16,)),
            dma((16,)),
        ],
        compiler_params=pltpu.CompilerParams(
            collective_id=0, has_side_effects=True, vmem_limit_bytes=63 * 1024 * 1024
        ),
    )(owner, grad_partial, momentum)
    return pl.pallas_call(
        hand_over,
        out_shape=(fresh, update),
        in_specs=[anywhere] * 3,
        out_specs=[anywhere] * 2,
        scratch_shapes=[
            pltpu.SMEM((LAYERS,), jnp.int32),
            pltpu.VMEM((CAP, ROWS, COLS), f32),
            pltpu.VMEM((OWNERS * CAP, BLOCK, COLS), f32),
            pltpu.VMEM((LAYERS, BLOCK, COLS), f32),
            dma((5,)),
        ],
        compiler_params=pltpu.CompilerParams(vmem_limit_bytes=63 * 1024 * 1024),
    )(owner, *held)


def solution(mesh):
    placed = (P("expert", None, None, "dp"), P("expert", None, "dp"), P())
    return jax.shard_map(
        on_device,
        mesh=mesh,
        in_specs=placed,
        out_specs=(P("expert", None, "dp"), P(None, "expert", "dp")),
        check_vma=False,
    )
```
